32 devices in a mesh: groups: 2 (over x), seq: 16 (over z, y, core).
Axes of the slice: x: 2, y: 2, z: 4, core: 2. Of those that a mesh axis runs over, the one named last changes fastest.
Arguments:
- tokens: int32 [16384], P(('groups', 'seq')), parts along dimension 0, may hold values from 0 to 3
- dilations: int32 [2], replicated, may hold values from 1 to 64, as said below
- embedding: bfloat16 [4, 512], replicated, may hold values from -6 to 6
- norm_gain: float32 [2, 512], replicated, may hold values from 0.1 to 1.9
- conv_taps: float32 [2, 3, 512], replicated, may hold values from -3 to 3
- w_up: bfloat16 [2, 512, 512], replicated, may hold values from -0.25 to 0.25
- w_gate: bfloat16 [2, 512, 512], replicated, may hold values from -0.25 to 0.25
- w_out: bfloat16 [2, 512, 512], replicated, may hold values from -0.25 to 0.25
- cotangent: bfloat16 [16384, 512], P(('groups', 'seq')), parts along dimension 0, may hold values from -6 to 6
Outputs:
- grad_up: float32 [4, 512, 512], P('groups', None, 'seq'), parts along dimension 0
- grad_gate: float32 [4, 512, 512], P('groups', None, 'seq'), parts along dimension 0
- grad_out: float32 [4, 512, 512], P('groups', None, 'seq'), parts along dimension 0
- grad_taps: float32 [4, 3, 512], P('groups'), parts along dimension 0
- grad_gain: float32 [4, 512], P('groups'), parts along dimension 0
- grad_embed: float32 [8, 512], P('groups'), parts along dimension 0
The draws below stay inside these ranges and needn't reach their ends.
There are 2 independent parts, one for each index of `groups`. The reference program is written for one: setup_inputs(seed, part) draws one part's arguments, and reference() takes and returns one part's arrays. A program takes and returns all parts, laid end to end along the dimension named above; an argument that names none is the same for every part. Nothing has to cross between parts.
Inputs may be any that keep to these rules, and one draw needn't show every extreme that they name: `dilations`: at least one block has dilation exactly 64.
All inputs are finite; a program needn't handle non-finite values.
Results may differ from the reference program's by a relative error of at most 0.014.
Values may be sent and summed in bfloat16 or wider, within the bound.
A program may use at most 64 MiB of HBM per device.

```python
import jax
import jax.numpy as jnp
from jax import lax

C = 512
LAYERS = 2
DMAX = 64
SEQLEN = 8192


def draw_dilations(key, part):
    key = jax.random.fold_in(key, 7)
    key_one, key_two = jax.random.split(key)
    drawn = jax.random.randint(key_one, (LAYERS,), 1, DMAX)
    chosen = jax.random.randint(key_two, (), 0, LAYERS)
    return jnp.where(jnp.arange(LAYERS) == chosen, DMAX, drawn).astype(jnp.int32)


def touch_ends(entries, rng, least, largest):
    extent = entries.shape
    place = [jax.random.randint(jax.random.fold_in(rng, axis), (), 0, extent[axis]) for axis in range(len(extent))]
    entries = entries.at[tuple(place)].set(least)
    longest = extent.index(max(extent))
    place[longest] = (place[longest] + 1) % extent[longest]
    return entries.at[tuple(place)].set(largest)


def with_spikes(entries, rng, source, target, shards_of, factor):
    owner, partner = [(jnp.arange(entries.shape[position]) // (entries.shape[position] // shards_of)).reshape([-1 if axis == position else 1 for axis in range(entries.ndim)]) for position in (source, target)]
    chosen = jax.random.permutation(rng, shards_of)[partner]
    strong = (owner == chosen) | (owner == (partner + shards_of // 2) % shards_of)
    return jnp.where(strong, factor * entries, entries)


def steps_of(stream_key, extent, cuts, low, top_value):
    level, own = 1.0, jax.random.fold_in(stream_key, 6)
    for axis_at, shards_of in cuts:
        heights = jnp.exp(jax.random.uniform(jax.random.fold_in(own, axis_at), (shards_of,), jnp.float32, low / len(cuts), top_value / len(cuts)))
        level = level * jnp.repeat(heights, extent[axis_at] // shards_of).reshape([-1 if axis == axis_at else 1 for axis in range(len(extent))])
    return level


def scatter_about(key, shape, deviation, most, pieces=(), kind=jnp.bfloat16):
    entries = jax.random.normal(key, shape, jnp.float32) * deviation
    if len(pieces) > 0:
        entries = steps_of(key, shape, pieces, -0.22, 0.18) * entries
    return jnp.clip(entries, min=-most, max=most).astype(kind)


def gaussian_with(rng, extent, spread, reach, cuts, heavy, held_as=jnp.bfloat16):
    values = spread * jax.random.normal(rng, extent, jnp.float32)
    if cuts:
        values = values * steps_of(rng, extent, cuts, -0.22, 0.18)
    return jnp.clip(with_spikes(values, jax.random.fold_in(rng, 3), *heavy), -reach, reach).astype(held_as)


def setup_inputs(seed: int = 0, part: int = 0) -> dict:
    splits = jax.random.split(jax.random.key(seed), 10)
    part_splits = jax.random.split(jax.random.fold_in(splits[9], part), 10)
    tokens = touch_ends(jax.random.randint(part_splits[0], (SEQLEN,), 0, 4), jax.random.fold_in(part_splits[0], 1), 0, 3).astype(jnp.int32)
    dilations = draw_dilations(jax.random.fold_in(splits[9], 71), part)
    embedding = scatter_about(splits[2], (4, C), 1.0, 6.0)
    norm_gain = jnp.clip(1.0 + 0.18 * jax.random.normal(splits[3], (LAYERS, C), jnp.float32), 0.1, 1.9)
    conv_taps = scatter_about(splits[4], (LAYERS, 3, C), 0.6, 3.0, (), jnp.float32)
    w_up = scatter_about(splits[5], (LAYERS, C, C), C ** -0.5, 0.25)
    w_gate = scatter_about(splits[6], (LAYERS, C, C), C ** -0.5, 0.25)
    w_out = scatter_about(splits[7], (LAYERS, C, C), C ** -0.5, 0.25)
    cotangent = gaussian_with(part_splits[8], (SEQLEN, C), 1.0, 6.0, ((0, 16),), (0, 1, 16, 2.0))
    return dict(tokens=tokens, dilations=dilations, embedding=embedding, norm_gain=norm_gain, conv_taps=conv_taps, w_up=w_up, w_gate=w_gate, w_out=w_out, cotangent=cotangent)


EPSILON = 1e-06

def shifted(padded, tapset, dilation, row_count, direction):
    summed = jnp.zeros((row_count, padded.shape[1]), jnp.float32)
    for offset in range(3):
        begin = (DMAX + direction * (offset - 1) * dilation).astype(jnp.int32)
        window = lax.dynamic_slice_in_dim(padded, begin, row_count, 0).astype(jnp.float32)
        summed = summed + tapset[offset][None, :] * window
    return summed

def reference(tokens, dilations, embedding, norm_gain, conv_taps, w_up, w_gate, w_out, cotangent):
    row_count = tokens.shape[0]
    one_hot = tokens[:, None] == jnp.arange(4, dtype=jnp.int32)[None, :]
    state = jnp.dot(one_hot.astype(jnp.bfloat16), embedding, preferred_element_type=jnp.float32).astype(jnp.bfloat16)
    saved = []
    for layer_at in range(LAYERS):
        dilation = dilations[layer_at]
        wide = state.astype(jnp.float32)
        inverse = lax.rsqrt(lax.optimization_barrier(jnp.mean(wide * wide, axis=-1, keepdims=True)) + EPSILON)
        unit = wide * inverse
        normed = (unit * norm_gain[layer_at][None, :]).astype(jnp.bfloat16)
        padded = jnp.pad(normed, ((DMAX, DMAX), (0, 0)))
        mixed = shifted(padded, conv_taps[layer_at], dilation, row_count, 1).astype(jnp.bfloat16)
        partner = jnp.flip(normed, 0)
        upward = jnp.dot(mixed, w_up[layer_at], preferred_element_type=jnp.float32)
        gate_sig = jax.nn.sigmoid(jnp.dot(partner, w_gate[layer_at], preferred_element_type=jnp.float32))
        hidden = (upward * gate_sig).astype(jnp.bfloat16)
        saved.append((unit, inverse, padded, mixed, partner, upward, gate_sig, hidden, dilation))
        if layer_at + 1 < LAYERS:
            state = (wide + jnp.dot(hidden, w_out[layer_at], preferred_element_type=jnp.float32)).astype(jnp.bfloat16)
    gradient = cotangent.astype(jnp.float32)
    up_list, gate_list, out_list, tap_list, gain_list = ([], [], [], [], [])
    for layer_at in reversed(range(LAYERS)):
        unit, inverse, padded, mixed, partner, upward, gate_sig, hidden, dilation = saved[layer_at]
        grad_low = gradient.astype(jnp.bfloat16)
        out_list.append(jnp.dot(hidden.T, grad_low, preferred_element_type=jnp.float32))
        grad_hidden = jnp.dot(grad_low, w_out[layer_at].T, preferred_element_type=jnp.float32)
        grad_upward = (grad_hidden * gate_sig).astype(jnp.bfloat16)
        grad_logit = (grad_hidden * upward * gate_sig * (1.0 - gate_sig)).astype(jnp.bfloat16)
        up_list.append(jnp.dot(mixed.T, grad_upward, preferred_element_type=jnp.float32))
        gate_list.append(jnp.dot(partner.T, grad_logit, preferred_element_type=jnp.float32))
        grad_mixed = jnp.dot(grad_upward, w_up[layer_at].T, preferred_element_type=jnp.float32).astype(jnp.bfloat16)
        grad_partner = jnp.dot(grad_logit, w_gate[layer_at].T, preferred_element_type=jnp.float32).astype(jnp.bfloat16)
        grad_pad = jnp.pad(grad_mixed, ((DMAX, DMAX), (0, 0)))
        grad_normed = shifted(grad_pad, conv_taps[layer_at], dilation, row_count, -1) + jnp.flip(grad_partner, 0).astype(jnp.float32)
        tap_rows = []
        for offset in range(3):
            begin = (DMAX + (offset - 1) * dilation).astype(jnp.int32)
            window = lax.dynamic_slice_in_dim(padded, begin, row_count, 0).astype(jnp.float32)
            tap_rows.append(lax.optimization_barrier(jnp.sum(grad_mixed.astype(jnp.float32) * window, axis=0)))
        tap_list.append(jnp.stack(tap_rows))
        gain_list.append(lax.optimization_barrier(jnp.sum(grad_normed * unit, axis=0)))
        grad_unit = grad_normed * norm_gain[layer_at][None, :]
        gradient = gradient + inverse * (grad_unit - unit * lax.optimization_barrier(jnp.mean(grad_unit * unit, axis=-1, keepdims=True)))
    grad_embed = jnp.dot(one_hot.astype(jnp.float32).T, gradient, preferred_element_type=jnp.float32, precision=lax.Precision.HIGHEST)
    return (jnp.stack(up_list[::-1]), jnp.stack(gate_list[::-1]), jnp.stack(out_list[::-1]), jnp.stack(tap_list[::-1]), jnp.stack(gain_list[::-1]), grad_embed)
```

```python
import functools

import jax
import jax.numpy as jnp
from jax import lax
from jax.experimental import pallas as pl
from jax.experimental.pallas import tpu as pltpu
from jax.sharding import PartitionSpec as P

DMAX = 64
EPSILON = 1e-06
F32 = jnp.float32
BF16 = jnp.bfloat16


def reduce_kernel(n, steps, m0, m1, m2, m3, small, out, small_out, acc, send, recv, ssend, srecv, sems):
    me = lax.axis_index("seq")
    width = m0.shape[0] // n
    bits = [lax.rem(lax.div(me, 1 << j), 2) for j in range(steps)]
    partners = [me + (1 - 2 * bits[j]) * (1 << j) for j in range(steps)]

    barrier = pltpu.get_barrier_semaphore()
    for j in range(steps):
        pl.semaphore_signal(
            barrier, inc=1, device_id={"seq": partners[j]}, device_id_type=pl.DeviceIdType.MESH
        )

    def whole_block(dest):
        rows = pl.ds(pl.multiple_of(dest * width, width), width)
        return jnp.concatenate([m[rows, :] for m in (m0, m1, m2, m3)], axis=0)

    small_out[...] = small[...]
    base = 0
    for j in range(steps):
        count = n >> (j + 1)
        bit = bits[j]

        def pack(q, carry, j=j, base=base, bit=bit):
            at = 2 * q + (1 - bit)
            block = whole_block(at) if j == 0 else acc[at]
            send[base + q] = block.astype(BF16)
            return carry

        lax.fori_loop(0, count, pack, 0)
        ssend[j] = small_out[...]
        if j == 0:
            pl.semaphore_wait(barrier, steps)
        big = pltpu.make_async_remote_copy(
            src_ref=send.at[pl.ds(base, count)],
            dst_ref=recv.at[pl.ds(base, count)],
            send_sem=sems.at[0, j],
            recv_sem=sems.at[1, j],
            device_id={"seq": partners[j]},
            device_id_type=pl.DeviceIdType.MESH,
        )
        little = pltpu.make_async_remote_copy(
            src_ref=ssend.at[j],
            dst_ref=srecv.at[j],
            send_sem=sems.at[2, j],
            recv_sem=sems.at[3, j],
            device_id={"seq": partners[j]},
            device_id_type=pl.DeviceIdType.MESH,
        )
        big.start()
        little.start()
        big.wait()
        little.wait()

        def fold(q, carry, j=j, base=base, bit=bit):
            at = 2 * q + bit
            block = whole_block(at) if j == 0 else acc[at]
            acc[q] = block + recv[base + q].astype(F32)
            return carry

        lax.fori_loop(0, count, fold, 0)
        small_out[...] = small_out[...] + srecv[j]
        base += count
    out[...] = acc[0]


def reduce_all(mats, small):
    n = lax.axis_size("seq")
    steps = n.bit_length() - 1
    width = mats[0].shape[0] // n
    cols = mats[0].shape[1]
    vmem = pl.BlockSpec(memory_space=pltpu.VMEM)
    return pl.pallas_call(
        functools.partial(reduce_kernel, n, steps),
        out_shape=(
            jax.ShapeDtypeStruct((4 * width, cols), F32),
            jax.ShapeDtypeStruct(small.shape, F32),
        ),
        in_specs=[vmem] * 5,
        out_specs=(vmem, vmem),
        scratch_shapes=[
            pltpu.VMEM((n // 2, 4 * width, cols), F32),
            pltpu.VMEM((n - 1, 4 * width, cols), BF16),
            pltpu.VMEM((n - 1, 4 * width, cols), BF16),
            pltpu.VMEM((steps,) + small.shape, F32),
            pltpu.VMEM((steps,) + small.shape, F32),
            pltpu.SemaphoreType.DMA((4, steps)),
        ],
        compiler_params=pltpu.CompilerParams(
            collective_id=0, has_side_effects=True, vmem_limit_bytes=48 * 1024 * 1024
        ),
    )(*mats, small)


def dot(a, b):
    return lax.dot_general(a, b, (((a.ndim - 1,), (0,)), ((), ())), preferred_element_type=F32)


def dot_t(a, b):
    return lax.dot_general(a, b, (((a.ndim - 1,), (1,)), ((), ())), preferred_element_type=F32)


def over_rows(a, b):
    return lax.dot_general(
        a.reshape(-1, a.shape[-1]),
        b.reshape(-1, b.shape[-1]),
        (((0,), (0,)), ((), ())),
        preferred_element_type=F32,
    )


def parts(a):
    high = a.astype(BF16)
    return high, (a - high.astype(F32)).astype(BF16)


def table_dot(table, w, transposed=False):
    high, low = parts(table)
    both = jnp.concatenate([high, low], axis=0)
    product = dot_t(both, w) if transposed else dot(both, w)
    return product[: table.shape[0]] + product[table.shape[0] :]


def look_up(hot, table):
    high, low = parts(table)
    return dot(jnp.concatenate([hot, hot], axis=-1), jnp.concatenate([high, low], axis=0))


def windows(rows, start, count, dilation):
    out = []
    for k in range(3):
        first = lax.dynamic_slice_in_dim(rows[0], start + (k - 1) * dilation, count, 0)
        second = lax.dynamic_slice_in_dim(rows[1], start - (k - 1) * dilation, count, 0)
        out.append(jnp.stack([first, second]))
    return out


def flipped(rows):
    size = rows.shape[0]
    at = lax.broadcasted_iota(jnp.int32, (size, size), 0)
    to = lax.broadcasted_iota(jnp.int32, (size, size), 1)
    return dot((at + to == size - 1).astype(BF16), rows).astype(BF16)


def per_device(tokens, dilations, embedding, norm_gain, conv_taps, w_up, w_gate, w_out, cotangent):
    n = lax.axis_size("seq")
    me = lax.axis_index("seq")
    rows = tokens.shape[0]
    half = rows // 2
    channels = embedding.shape[1]
    to_mirror = [(i, n - 1 - i) for i in range(n)]
    to_next = [(i, (i + 1) % n) for i in range(n)]
    to_beyond = [(i, (n - i) % n) for i in range(n)]

    tok_prev = lax.ppermute(tokens, "seq", to_next)
    tok_mirror = lax.ppermute(tokens, "seq", to_mirror)
    tok_beyond = lax.ppermute(tokens, "seq", to_beyond)
    cot_mirror = lax.ppermute(cotangent[half - DMAX :], "seq", to_mirror)
    cot_prev = lax.ppermute(cotangent[rows - DMAX :], "seq", to_next)
    cot_beyond = lax.ppermute(cotangent[:DMAX], "seq", to_beyond)

    edge = 3 * DMAX
    tok = jnp.stack(
        [
            jnp.concatenate([tok_prev[rows - edge :], tokens[: half + edge]]),
            jnp.flip(jnp.concatenate([tok_mirror[half - edge :], tok_beyond[:edge]])),
        ]
    )
    position = me * rows - edge + jnp.arange(half + 2 * edge, dtype=jnp.int32)
    inside = position >= 0
    bases = jnp.arange(4, dtype=jnp.int32)
    hot = ((tok[:, :, None] == bases) & inside[None, :, None]).astype(BF16)

    wide0 = embedding.astype(F32)
    inverse0 = lax.rsqrt(jnp.mean(wide0 * wide0, axis=-1, keepdims=True) + EPSILON)
    unit0 = wide0 * inverse0
    table = (unit0 * norm_gain[0]).astype(BF16)
    table_wide = table.astype(F32)
    tapped = (conv_taps[0][:, None, :] * table_wide[None]).reshape(12, channels)
    up_table = table_dot(tapped, w_up[0])
    gate_table = jax.nn.sigmoid(dot(table, w_gate[0]))

    d0, d1 = dilations[0], dilations[1]
    count1 = half + 4 * DMAX
    hot12 = jnp.concatenate(windows(hot, DMAX, count1, d0), axis=-1)
    hot_own = hot[:, DMAX : DMAX + count1]
    hot_partner = hot_own[::-1]
    upward0 = look_up(hot12, up_table)
    gate0 = look_up(hot_partner, gate_table)
    hidden0 = (upward0 * gate0).astype(BF16)
    wide = (dot(hot_own, embedding) + dot(hidden0, w_out[0])).astype(BF16).astype(F32)

    inverse = lax.rsqrt(jnp.mean(wide * wide, axis=-1, keepdims=True) + EPSILON)
    unit = wide * inverse
    normed = jnp.where(
        inside[None, DMAX : DMAX + count1, None], unit * norm_gain[1], 0.0
    ).astype(BF16)

    taps1 = conv_taps[1]
    count2 = half + 2 * DMAX
    shifted = windows(normed, DMAX, count2, d1)
    mixed = sum(taps1[k] * shifted[k].astype(F32) for k in range(3)).astype(BF16)
    partner = normed[::-1, DMAX : DMAX + count2]
    upward = dot(mixed, w_up[1])
    gate = jax.nn.sigmoid(dot(partner, w_gate[1]))
    hidden = (upward * gate).astype(BF16)

    cot_first = jnp.concatenate([cot_prev, cotangent[: half + DMAX]])
    cot_second = flipped(jnp.concatenate([cot_mirror, cot_beyond]))
    low = jnp.where(
        inside[None, 2 * DMAX : 2 * DMAX + count2, None],
        jnp.stack([cot_first, cot_second]),
        jnp.zeros((), BF16),
    )
    grad_hidden = dot_t(low, w_out[1])
    grad_upward = (grad_hidden * gate).astype(BF16)
    grad_logit = (grad_hidden * upward * gate * (1.0 - gate)).astype(BF16)
    own = slice(DMAX, DMAX + half)
    term_out1 = over_rows(low[:, own], hidden[:, own])
    term_up1 = over_rows(grad_upward[:, own], mixed[:, own])
    term_gate1 = over_rows(grad_logit[:, own], partner[:, own])
    grad_mixed = dot_t(grad_upward, w_up[1]).astype(BF16)
    grad_partner = dot_t(grad_logit[:, own], w_gate[1]).astype(BF16)

    moved = windows(grad_mixed, DMAX, half, -d1)
    grad_normed = sum(taps1[k] * moved[k].astype(F32) for k in range(3))
    grad_normed = grad_normed + grad_partner[::-1].astype(F32)
    mixed_own = grad_mixed[:, own].astype(F32)
    taps_term = jnp.stack(
        [jnp.sum(mixed_own * shifted[k][:, own].astype(F32), axis=(0, 1)) for k in range(3)]
    )
    unit_own = unit[:, 2 * DMAX : 2 * DMAX + half]
    inverse_own = inverse[:, 2 * DMAX : 2 * DMAX + half]
    gain_term = jnp.sum(grad_normed * unit_own, axis=(0, 1))[None]
    grad_unit = grad_normed * norm_gain[1]
    gradient = low[:, own].astype(F32) + inverse_own * (
        grad_unit - unit_own * jnp.mean(grad_unit * unit_own, axis=-1, keepdims=True)
    )

    low0, rest0 = parts(gradient)
    own0 = slice(2 * DMAX, 2 * DMAX + half)
    grad_hidden0 = dot_t(low0, w_out[0])
    gate_own = gate0[:, own0]
    grad_upward0 = grad_hidden0 * gate_own
    grad_logit0 = (grad_upward0 * upward0[:, own0] * (1.0 - gate_own)).astype(BF16)
    term_out0 = over_rows(low0, hidden0[:, own0])
    sum_up = over_rows(hot12[:, own0], grad_upward0.astype(BF16))
    sum_logit = over_rows(hot_partner[:, own0], grad_logit0)
    hot_here = hot_own[:, own0]
    sum_grad = over_rows(hot_here, low0) + over_rows(hot_here, rest0)

    small = jnp.concatenate([sum_up, sum_logit, sum_grad, taps_term, gain_term], axis=0)
    mats, small = reduce_all((term_out0, term_out1, term_up1, term_gate1), small)

    width = channels // n
    sum_up, sum_logit, sum_grad = small[:12], small[12:16], small[16:20]
    columns = jnp.concatenate([sum_up, sum_logit], axis=0)
    mine = lax.dynamic_slice_in_dim(columns, me * width, width, 1)
    exact = functools.partial(
        lax.dot_general,
        dimension_numbers=(((0,), (0,)), ((), ())),
        precision=lax.Precision.HIGHEST,
        preferred_element_type=F32,
    )
    out0, out1, up1, gate1 = [m.T for m in mats.reshape(4, width, channels)]
    grad_up = jnp.stack([exact(tapped, mine[:12]), up1])
    grad_gate = jnp.stack([exact(table_wide, mine[12:]), gate1])
    grad_out = jnp.stack([out0, out1])

    spread = table_dot(sum_up, w_up[0], True).reshape(3, 4, channels)
    grad_normed0 = jnp.sum(conv_taps[0][:, None, :] * spread, axis=0)
    grad_normed0 = grad_normed0 + table_dot(sum_logit, w_gate[0], True)
    grad_taps = jnp.stack([jnp.sum(spread * table_wide[None], axis=1), small[20:23]])
    grad_gain = jnp.stack([jnp.sum(grad_normed0 * unit0, axis=0), small[23]])
    grad_unit0 = grad_normed0 * norm_gain[0]
    grad_embed = sum_grad + inverse0 * (
        grad_unit0 - unit0 * jnp.mean(grad_unit0 * unit0, axis=-1, keepdims=True)
    )
    return (grad_up, grad_gate, grad_out, grad_taps, grad_gain, grad_embed)


def solution(mesh):
    in_specs = (P(("groups", "seq")), P(), P(), P(), P(), P(), P(), P(), P(("groups", "seq"), None))
    out_specs = (
        P("groups", None, "seq"),
        P("groups", None, "seq"),
        P("groups", None, "seq"),
        P("groups", None, None),
        P("groups", None),
        P("groups", None),
    )
    return jax.shard_map(
        per_device, mesh=mesh, in_specs=in_specs, out_specs=out_specs, check_vma=False
    )
```

```python
import functools

import jax
import jax.numpy as jnp
from jax import lax
from jax.experimental import pallas as pl
from jax.experimental.pallas import tpu as pltpu
from jax.sharding import PartitionSpec as P

DMAX = 64
EPSILON = 1e-06
F32 = jnp.float32
BF16 = jnp.bfloat16


def turned(a, b):
    return lax.dot_general(a, b, (((0,), (0,)), ((), ())), preferred_element_type=F32)


def dot(a, b):
    return jnp.dot(a, b, preferred_element_type=F32)


def dot_t(a, b):
    return lax.dot_general(a, b, (((1,), (1,)), ((), ())), preferred_element_type=F32)


def parts(a):
    high = a.astype(BF16)
    return high, (a - high.astype(F32)).astype(BF16)


def table_dot(table, w, transposed=False):
    high, low = parts(table)
    both = jnp.concatenate([high, low], axis=0)
    product = dot_t(both, w) if transposed else dot(both, w)
    return product[: table.shape[0]] + product[table.shape[0] :]


class Halving:
    def __init__(self, n, order, me, mats, acc, send, recv, sems):
        self.n, self.order, self.me, self.mats = n, order, me, mats
        self.acc, self.send, self.recv, self.sems = acc, send, recv, sems
        self.left = sorted(order)
        self.base = 0

    def plan(self, j):
        bit_at = self.order[j]
        at = self.left.index(bit_at)
        bit = lax.rem(lax.div(self.me, 1 << bit_at), 2)
        return at, bit, self.me + (1 - 2 * bit) * (1 << bit_at), self.n >> (j + 1)

    def block(self, j, q, at, bit):
        low = 1 << at
        index = lax.div(q, low) * (2 * low) + bit * low + lax.rem(q, low)
        if j > 0:
            return self.acc[index]
        width = self.mats[0].shape[0] // self.n
        rows = pl.ds(pl.multiple_of(index * width, width), width)
        return jnp.concatenate([m[rows, :] for m in self.mats], axis=0)

    def copy(self, j):
        at, bit, partner, count = self.plan(j)
        where = pl.ds(self.base, count)
        return pltpu.make_async_remote_copy(
            src_ref=self.send.at[where],
            dst_ref=self.recv.at[where],
            send_sem=self.sems.at[0, j],
            recv_sem=self.sems.at[1, j],
            device_id={"seq": partner},
            device_id_type=pl.DeviceIdType.MESH,
        )

    def start(self, j):
        at, bit, partner, count = self.plan(j)
        base = self.base

        def pack(q, carry):
            self.send[base + q] = self.block(j, q, at, 1 - bit).astype(self.send.dtype)
            return carry

        lax.fori_loop(0, count, pack, 0)
        self.copy(j).start()

    def finish(self, j):
        at, bit, partner, count = self.plan(j)
        base = self.base
        self.copy(j).wait()

        def fold(q, carry):
            self.acc[q] = self.block(j, q, at, bit) + self.recv[base + q].astype(F32)
            return carry

        lax.fori_loop(0, count, fold, 0)
        self.base += count
        self.left.remove(self.order[j])


def kernel(
    n, steps, dil, codes, emb, gain, taps, up_w, gate_w, out_w, cot,
    out_a, out_b, small_out,
    low_s, second_s, unit_s, inv_s, norm_s, mixed_s, partner_s, hidden_s, gu_s, gl_s, gm_s, gp_s,
    low0_s, hidden0_s, m_out1, m_up1, m_gate1, m_out0,
    acc_a, send_a, recv_a, acc_b, send_b, recv_b, ssend, srecv,
    sems_a, sems_b, sems_s, sems_c,
):
    me = lax.axis_index("seq")
    rows, channels = cot.shape
    half = rows // 2
    full, part = half + 4 * DMAX, half + 2 * DMAX
    mirror = n - 1 - me
    following = lax.rem(me + 1, n)
    previous = lax.rem(me + n - 1, n)
    beyond = lax.rem(n - me, n)
    alone = beyond == me

    barrier = pltpu.get_barrier_semaphore()

    def greet(device):
        pl.semaphore_signal(
            barrier, inc=1, device_id={"seq": device}, device_id_type=pl.DeviceIdType.MESH
        )

    for j in range(steps):
        greet(me + (1 - 2 * lax.rem(lax.div(me, 1 << j), 2)) * (1 << j))
    greet(mirror)
    greet(following)
    greet(previous)

    @pl.when(jnp.logical_not(alone))
    def _():
        greet(beyond)

    pl.semaphore_wait(barrier, steps + 4 - jnp.where(alone, 1, 0))

    def send_rows(src, dst, at, device):
        return pltpu.make_async_remote_copy(
            src_ref=src, dst_ref=dst, send_sem=sems_c.at[0, at], recv_sem=sems_c.at[1, at],
            device_id={"seq": device}, device_id_type=pl.DeviceIdType.MESH,
        )

    near = half + DMAX
    to_mirror = send_rows(cot.at[pl.ds(half - DMAX, near)], second_s.at[pl.ds(0, near)], 0, mirror)
    to_next = send_rows(cot.at[pl.ds(rows - DMAX, DMAX)], low_s.at[pl.ds(0, DMAX)], 1, following)
    to_beyond = send_rows(cot.at[pl.ds(0, DMAX)], second_s.at[pl.ds(near, DMAX)], 2, beyond)
    to_mirror.start()
    to_next.start()

    @pl.when(alone)
    def _():
        own_copy = pltpu.make_async_copy(
            cot.at[pl.ds(0, DMAX)], second_s.at[pl.ds(near, DMAX)], sems_c.at[0, 3]
        )
        own_copy.start()
        own_copy.wait()

    @pl.when(jnp.logical_not(alone))
    def _():
        to_beyond.start()

    low_s[DMAX:part, :] = cot[0:near, :]

    embedded = emb[...]
    wide0 = embedded.astype(F32)
    unit0 = wide0 * lax.rsqrt(jnp.mean(wide0 * wide0, axis=-1, keepdims=True) + EPSILON)
    table = (unit0 * gain[0:1, :]).astype(BF16)
    table_wide = table.astype(F32)
    tapped = jnp.concatenate([taps[0, k : k + 1, :] * table_wide for k in range(3)], axis=0)
    tapped = jnp.concatenate([tapped, jnp.zeros((4, channels), F32)], axis=0)
    up_high, up_low = parts(table_dot(tapped, up_w[0]))
    gates = jax.nn.sigmoid(dot(jnp.concatenate([table_wide] * 4, axis=0).astype(BF16), gate_w[0]))
    row_of = lax.broadcasted_iota(jnp.int32, (16, channels), 0)
    gate_high, gate_low = parts(jnp.where(row_of >= 12, gates, 0.0))
    up_table = jnp.concatenate([up_high, up_low], axis=0)
    gate_table = jnp.concatenate([gate_high, gate_low], axis=0)
    embed_table = jnp.where(
        (row_of >= 4) & (row_of < 8), jnp.concatenate([wide0] * 4, axis=0), 0.0
    ).astype(BF16)
    hot_rows = lax.broadcasted_iota(jnp.int32, (16, 128), 0)

    def hot_at(start):
        code = codes[:, pl.ds(pl.multiple_of(start, 128), 128)]
        return jnp.where(code == lax.rem(hot_rows, 4), 1.0, 0.0)

    def block0(hot):
        two = jnp.concatenate([hot, hot], axis=0).astype(BF16)
        return turned(two, up_table), turned(two, gate_table)

    first_row = lax.broadcasted_iota(jnp.int32, (128, 1), 0)

    def forward0(c, carry):
        start = pl.multiple_of(c * 128, 128)
        hot = hot_at(start)
        upward0, gate0 = block0(hot)
        hidden0 = (upward0 * gate0).astype(BF16)
        wide = turned(hot.astype(BF16), embed_table) + dot(hidden0, out_w[0])
        wide = wide.astype(BF16).astype(F32)
        inverse = lax.rsqrt(jnp.mean(wide * wide, axis=-1, keepdims=True) + EPSILON)
        unit = wide * inverse
        place = me * rows - 2 * DMAX + lax.rem(start, full) + first_row
        normed = jnp.where(place >= 0, unit * gain[1:2, :], 0.0).astype(BF16)
        at = pl.ds(start, 128)
        unit_s[at, :] = unit
        inv_s[at, :] = jnp.broadcast_to(inverse, (128, 128))
        norm_s[at, :] = normed
        return carry

    lax.fori_loop(0, 2 * full // 128, forward0, 0)

    to_mirror.wait()
    to_next.wait()

    @pl.when(jnp.logical_not(alone))
    def _():
        to_beyond.wait()

    up = lax.broadcasted_iota(jnp.int32, (part, part), 0)
    down = lax.broadcasted_iota(jnp.int32, (part, part), 1)
    flip = jnp.where(up + down == part - 1, 1.0, 0.0).astype(BF16)
    edge_row = lax.broadcasted_iota(jnp.int32, (DMAX, 1), 0)
    within = me * rows - DMAX + edge_row >= 0
    low_s[part : 2 * part, :] = dot(flip, second_s[...]).astype(BF16)
    for p in range(2):
        edge = low_s[p * part : p * part + DMAX, :].astype(F32)
        low_s[p * part : p * part + DMAX, :] = jnp.where(within, edge, 0.0).astype(BF16)

    d1 = dil[1]
    tap = [taps[1, k : k + 1, :] for k in range(3)]

    to_row = lax.broadcasted_iota(jnp.int32, (128, 256), 0)
    from_row = lax.broadcasted_iota(jnp.int32, (128, 256), 1)
    distance = from_row - to_row - DMAX

    def shifted(ref, at, offset):
        window = ref[pl.ds(pl.multiple_of(at - DMAX, 64), 256), :]
        move = jnp.where(distance == offset, 1.0, 0.0).astype(BF16)
        return dot(move, window)

    def middle(c, carry):
        p = lax.div(c, part // 128)
        r0 = lax.rem(c, part // 128) * 128
        sign = 1 - 2 * p
        begin = p * full + DMAX + r0
        mixed = tap[0] * shifted(norm_s, begin, -sign * d1)
        mixed = mixed + tap[1] * norm_s[pl.ds(pl.multiple_of(begin, 64), 128), :].astype(F32)
        mixed = (mixed + tap[2] * shifted(norm_s, begin, sign * d1)).astype(BF16)
        other = pl.multiple_of((1 - p) * full + DMAX + r0, 64)
        partner = norm_s[pl.ds(other, 128), :]
        at = pl.ds(pl.multiple_of(c * 128, 128), 128)
        upward = dot(mixed, up_w[1])
        gate = jax.nn.sigmoid(dot(partner, gate_w[1]))
        grad_hidden = dot_t(low_s[at, :], out_w[1])
        gated = grad_hidden * gate
        gu = gated.astype(BF16)
        gl = (gated * upward * (1.0 - gate)).astype(BF16)
        mixed_s[at, :] = mixed
        partner_s[at, :] = partner
        hidden_s[at, :] = (upward * gate).astype(BF16)
        gu_s[at, :] = gu
        gl_s[at, :] = gl
        gm_s[at, :] = dot_t(gu, up_w[1]).astype(BF16)
        gp_s[at, :] = dot_t(gl, gate_w[1]).astype(BF16)
        return carry

    lax.fori_loop(0, 2 * part // 128, middle, 0)

    def own(ref, cols=slice(None)):
        return jnp.concatenate(
            [ref[DMAX : DMAX + half, cols], ref[part + DMAX : part + DMAX + half, cols]], axis=0
        )

    def rows_into(mat, left, right, pick):
        whole = pick(right)
        for c in range(channels // 256):
            cols = slice(c * 256, c * 256 + 256)
            mat[cols, :] = turned(pick(left, cols), whole)

    rows_into(m_out1, low_s, hidden_s, own)
    rows_into(m_up1, gu_s, mixed_s, own)
    rows_into(m_gate1, gl_s, partner_s, own)

    order_a = list(range(steps))
    order_b = [0] + order_a[2:] + [1]
    first = Halving(n, order_a, me, (m_out1, m_up1, m_gate1), acc_a, send_a, recv_a, sems_a)
    first.start(0)

    small_out[...] = jnp.zeros_like(small_out)

    def backward(c, carry):
        p = lax.div(c, half // 128)
        r0 = lax.rem(c, half // 128) * 128
        sign = 1 - 2 * p
        mine = p * part + DMAX + r0
        mine_at = pl.ds(pl.multiple_of(mine, 64), 128)
        here = p * full + 2 * DMAX + r0
        here_at = pl.ds(pl.multiple_of(here, 64), 128)
        grad_mixed = gm_s[mine_at, :].astype(F32)
        grad_normed = tap[0] * shifted(gm_s, mine, sign * d1)
        grad_normed = grad_normed + tap[1] * grad_mixed
        grad_normed = grad_normed + tap[2] * shifted(gm_s, mine, -sign * d1)
        other = pl.multiple_of((1 - p) * part + DMAX + r0, 64)
        grad_normed = grad_normed + gp_s[pl.ds(other, 128), :].astype(F32)
        unit = unit_s[here_at, :]
        sums = [
            jnp.sum(grad_mixed * shifted(norm_s, here, -sign * d1), axis=0, keepdims=True),
            jnp.sum(grad_mixed * norm_s[here_at, :].astype(F32), axis=0, keepdims=True),
            jnp.sum(grad_mixed * shifted(norm_s, here, sign * d1), axis=0, keepdims=True),
            jnp.sum(grad_normed * unit, axis=0, keepdims=True),
            jnp.zeros((4, channels), F32),
        ]
        grad_unit = grad_normed * gain[1:2, :]
        average = jnp.mean(grad_unit * unit, axis=-1, keepdims=True)
        gradient = low_s[mine_at, :].astype(F32) + inv_s[here_at, 0:1] * (
            grad_unit - unit * average
        )
        low0, rest0 = parts(gradient)
        grad_hidden0 = dot_t(low0, out_w[0])
        hot = hot_at(here)
        upward0, gate0 = block0(hot)
        gated = grad_hidden0 * gate0
        gu0 = gated.astype(BF16)
        gl0 = (gated * upward0 * (1.0 - gate0)).astype(BF16)
        hot_up = jnp.where(hot_rows < 12, hot, 0.0).astype(BF16)
        hot_gate = jnp.where(hot_rows < 12, 0.0, hot).astype(BF16)
        hot16 = hot.astype(BF16)
        small_out[0:16, :] += dot(hot_up, gu0) + dot(hot_gate, gl0)
        small_out[16:24, :] += (dot(hot16, low0) + dot(hot16, rest0))[0:8]
        small_out[24:32, :] += jnp.concatenate(sums, axis=0)
        at = pl.ds(pl.multiple_of(c * 128, 128), 128)
        low0_s[at, :] = low0
        hidden0_s[at, :] = (upward0 * gate0).astype(BF16)
        return carry

    lax.fori_loop(0, 2 * half // 128, backward, 0)

    first.finish(0)
    first.start(1)
    rows_into(m_out0, low0_s, hidden0_s, lambda ref, cols=slice(None): ref[:, cols])
    second = Halving(n, order_b, me, (m_out0,), acc_b, send_b, recv_b, sems_b)

    def small_copy(j):
        partner = second.plan(j)[2]
        return pltpu.make_async_remote_copy(
            src_ref=ssend.at[j], dst_ref=srecv.at[j],
            send_sem=sems_s.at[0, j], recv_sem=sems_s.at[1, j],
            device_id={"seq": partner}, device_id_type=pl.DeviceIdType.MESH,
        )

    for j in range(steps):
        ssend[j] = small_out[...]
        small_copy(j).start()
        second.start(j)
        if j + 1 < steps:
            if j > 0:
                first.start(j + 1)
            first.finish(j + 1) if j == 0 else None
        small_copy(j).wait()
        small_out[...] = small_out[...] + srecv[j]
        second.finish(j)
        if 0 < j and j + 1 < steps:
            first.finish(j + 1)
    out_a[...] = acc_a[0]
    out_b[...] = acc_b[0]


def fused(dilations, codes, embedding, norm_gain, conv_taps, w_up, w_gate, w_out, cotangent):
    n = lax.axis_size("seq")
    steps = n.bit_length() - 1
    rows, channels = cotangent.shape
    half = rows // 2
    full, part = 2 * (half + 4 * DMAX), 2 * (half + 2 * DMAX)
    width = channels // n
    vmem = pl.BlockSpec(memory_space=pltpu.VMEM)

    def wide(count, kind=F32, cols=channels):
        return pltpu.VMEM((count, cols), kind)

    def buffers(mats):
        return [
            pltpu.VMEM((n // 2, mats * width, channels), F32),
            pltpu.VMEM((n - 1, mats * width, channels), BF16 if mats * width % 16 == 0 else F32),
            pltpu.VMEM((n - 1, mats * width, channels), BF16 if mats * width % 16 == 0 else F32),
        ]

    sems = pltpu.SemaphoreType.DMA
    return pl.pallas_call(
        functools.partial(kernel, n, steps),
        out_shape=(
            jax.ShapeDtypeStruct((3 * width, channels), F32),
            jax.ShapeDtypeStruct((width, channels), F32),
            jax.ShapeDtypeStruct((32, channels), F32),
        ),
        in_specs=[pl.BlockSpec(memory_space=pltpu.SMEM)] + [vmem] * 8,
        out_specs=(vmem,) * 3,
        scratch_shapes=[
            wide(part, BF16), wide(part // 2, BF16),
            wide(full), wide(full, F32, 128), wide(full, BF16),
            *[wide(part, BF16) for _ in range(5)],
            wide(part, BF16), wide(part, BF16),
            wide(2 * half, BF16), wide(2 * half, BF16),
            *[wide(channels) for _ in range(4)],
            *buffers(3), *buffers(1),
            pltpu.VMEM((steps, 32, channels), F32), pltpu.VMEM((steps, 32, channels), F32),
            sems((2, steps)), sems((2, steps)), sems((2, steps)), sems((2, 4)),
        ],
        compiler_params=pltpu.CompilerParams(
            collective_id=0, has_side_effects=True, vmem_limit_bytes=56 * 1024 * 1024
        ),
    )(dilations, codes, embedding, norm_gain, conv_taps, w_up, w_gate, w_out, cotangent)


def per_device(tokens, dilations, embedding, norm_gain, conv_taps, w_up, w_gate, w_out, cotangent):
    n = lax.axis_size("seq")
    me = lax.axis_index("seq")
    rows = tokens.shape[0]
    half = rows // 2
    channels = embedding.shape[1]
    to_mirror = [(i, n - 1 - i) for i in range(n)]
    to_next = [(i, (i + 1) % n) for i in range(n)]
    to_beyond = [(i, (n - i) % n) for i in range(n)]

    tok_prev = lax.ppermute(tokens, "seq", to_next)
    tok_mirror = lax.ppermute(tokens, "seq", to_mirror)
    tok_beyond = lax.ppermute(tokens, "seq", to_beyond)
    edge = 3 * DMAX
    tok = jnp.stack(
        [
            jnp.concatenate([tok_prev[rows - edge :], tokens[: half + edge]]),
            jnp.flip(jnp.concatenate([tok_mirror[half - edge :], tok_beyond[:edge]])),
        ]
    )
    position = me * rows - edge + jnp.arange(half + 2 * edge, dtype=jnp.int32)
    inside = position >= 0
    tok = jnp.where(inside[None], tok, -1)
    d0 = dilations[0]
    count1 = half + 4 * DMAX
    codes = []
    for k in range(3):
        shift = (k - 1) * d0
        codes.append(
            jnp.concatenate(
                [
                    lax.dynamic_slice_in_dim(tok[0], DMAX + shift, count1, 0),
                    lax.dynamic_slice_in_dim(tok[1], DMAX - shift, count1, 0),
                ]
            )
        )
    codes.append(tok[::-1, DMAX : DMAX + count1].reshape(-1))
    codes = jnp.repeat(jnp.stack(codes), 4, axis=0)
    mats, mat_b, small = fused(
        dilations, codes, embedding, norm_gain, conv_taps, w_up, w_gate, w_out, cotangent
    )

    wide0 = embedding.astype(F32)
    inverse0 = lax.rsqrt(jnp.mean(wide0 * wide0, axis=-1, keepdims=True) + EPSILON)
    unit0 = wide0 * inverse0
    table_wide = (unit0 * norm_gain[0]).astype(BF16).astype(F32)
    tapped = (conv_taps[0][:, None, :] * table_wide[None]).reshape(12, channels)

    width = channels // n
    sum_up, sum_logit, sum_grad = small[:12], small[12:16], small[20:24]
    columns = jnp.concatenate([sum_up, sum_logit], axis=0)
    mine = lax.dynamic_slice_in_dim(columns, me * width, width, 1)
    exact = functools.partial(
        lax.dot_general,
        dimension_numbers=(((0,), (0,)), ((), ())),
        precision=lax.Precision.HIGHEST,
        preferred_element_type=F32,
    )
    out0 = mat_b.T
    out1, up1, gate1 = [m.T for m in mats.reshape(3, width, channels)]
    grad_up = jnp.stack([exact(tapped, mine[:12]), up1])
    grad_gate = jnp.stack([exact(table_wide, mine[12:]), gate1])
    grad_out = jnp.stack([out0, out1])

    spread = table_dot(sum_up, w_up[0], True).reshape(3, 4, channels)
    grad_normed0 = jnp.sum(conv_taps[0][:, None, :] * spread, axis=0)
    grad_normed0 = grad_normed0 + table_dot(sum_logit, w_gate[0], True)
    grad_taps = jnp.stack([jnp.sum(spread * table_wide[None], axis=1), small[24:27]])
    grad_gain = jnp.stack([jnp.sum(grad_normed0 * unit0, axis=0), small[27]])
    grad_unit0 = grad_normed0 * norm_gain[0]
    grad_embed = sum_grad + inverse0 * (
        grad_unit0 - unit0 * jnp.mean(grad_unit0 * unit0, axis=-1, keepdims=True)
    )
    return (grad_up, grad_gate, grad_out, grad_taps, grad_gain, grad_embed)


def solution(mesh):
    in_specs = (P(("groups", "seq")), P(), P(), P(), P(), P(), P(), P(), P(("groups", "seq"), None))
    out_specs = (
        P("groups", None, "seq"),
        P("groups", None, "seq"),
        P("groups", None, "seq"),
        P("groups", None, None),
        P("groups", None),
        P("groups", None),
    )
    return jax.shard_map(
        per_device, mesh=mesh, in_specs=in_specs, out_specs=out_specs, check_vma=False
    )
```

```python
import functools

import jax
import jax.numpy as jnp
from jax import lax
from jax.experimental import pallas as pl
from jax.experimental.pallas import tpu as pltpu
from jax.sharding import PartitionSpec as P

DMAX = 64
EPSILON = 1e-06
F32 = jnp.float32
BF16 = jnp.bfloat16


def turned(a, b):
    return lax.dot_general(a, b, (((0,), (0,)), ((), ())), preferred_element_type=F32)


def dot(a, b):
    return jnp.dot(a, b, preferred_element_type=F32)


def dot_t(a, b):
    return lax.dot_general(a, b, (((1,), (1,)), ((), ())), preferred_element_type=F32)


def parts(a):
    high = a.astype(BF16)
    return high, (a - high.astype(F32)).astype(BF16)


def table_dot(table, w, transposed=False):
    high, low = parts(table)
    both = jnp.concatenate([high, low], axis=0)
    product = dot_t(both, w) if transposed else dot(both, w)
    return product[: table.shape[0]] + product[table.shape[0] :]


class Halving:
    def __init__(self, n, order, me, mats, acc, send, recv, sems):
        self.n, self.order, self.me, self.mats = n, order, me, mats
        self.acc, self.send, self.recv, self.sems = acc, send, recv, sems
        self.left = sorted(order)
        self.base = 0

    def plan(self, j):
        bit_at = self.order[j]
        at = self.left.index(bit_at)
        bit = lax.rem(lax.div(self.me, 1 << bit_at), 2)
        return at, bit, self.me + (1 - 2 * bit) * (1 << bit_at), self.n >> (j + 1)

    def block(self, j, q, at, bit):
        low = 1 << at
        index = lax.div(q, low) * (2 * low) + bit * low + lax.rem(q, low)
        if j > 0:
            return self.acc[index]
        width = self.mats[0].shape[0] // self.n
        rows = pl.ds(pl.multiple_of(index * width, width), width)
        return jnp.concatenate([m[rows, :] for m in self.mats], axis=0)

    def copy(self, j):
        at, bit, partner, count = self.plan(j)
        where = pl.ds(self.base, count)
        return pltpu.make_async_remote_copy(
            src_ref=self.send.at[where],
            dst_ref=self.recv.at[where],
            send_sem=self.sems.at[0, j],
            recv_sem=self.sems.at[1, j],
            device_id={"seq": partner},
            device_id_type=pl.DeviceIdType.MESH,
        )

    def start(self, j):
        at, bit, partner, count = self.plan(j)
        base = self.base

        def pack(q, carry):
            self.send[base + q] = self.block(j, q, at, 1 - bit).astype(self.send.dtype)
            return carry

        lax.fori_loop(0, count, pack, 0)
        self.copy(j).start()

    def finish(self, j):
        at, bit, partner, count = self.plan(j)
        base = self.base
        self.copy(j).wait()

        def fold(q, carry):
            self.acc[q] = self.block(j, q, at, bit) + self.recv[base + q].astype(F32)
            return carry

        lax.fori_loop(0, count, fold, 0)
        self.base += count
        self.left.remove(self.order[j])


def kernel(
    n, steps, dil, codes, emb, gain, taps, up_w, gate_w, out_w, cot,
    out_a, out_b, out_c, out_taps, out_gain, out_embed,
    small_out,
    low_s, second_s, unit_s, inv_s, norm_s, mixed_s, partner_s, hidden_s, gu_s, gl_s, gm_s, gp_s,
    low0_s, hidden0_s, m_out1, m_up1, m_gate1, m_out0,
    acc_a, send_a, recv_a, acc_b, send_b, recv_b, ssend, srecv,
    sems_a, sems_b, sems_s, sems_c,
):
    me = lax.axis_index("seq")
    rows, channels = cot.shape
    half = rows // 2
    full, part = half + 4 * DMAX, half + 2 * DMAX
    mirror = n - 1 - me
    following = lax.rem(me + 1, n)
    previous = lax.rem(me + n - 1, n)
    beyond = lax.rem(n - me, n)
    alone = beyond == me

    barrier = pltpu.get_barrier_semaphore()

    def greet(device):
        pl.semaphore_signal(
            barrier, inc=1, device_id={"seq": device}, device_id_type=pl.DeviceIdType.MESH
        )

    for j in range(steps):
        greet(me + (1 - 2 * lax.rem(lax.div(me, 1 << j), 2)) * (1 << j))
    greet(mirror)
    greet(following)
    greet(previous)

    @pl.when(jnp.logical_not(alone))
    def _():
        greet(beyond)

    pl.semaphore_wait(barrier, steps + 4 - jnp.where(alone, 1, 0))

    def send_rows(src, dst, at, device):
        return pltpu.make_async_remote_copy(
            src_ref=src, dst_ref=dst, send_sem=sems_c.at[0, at], recv_sem=sems_c.at[1, at],
            device_id={"seq": device}, device_id_type=pl.DeviceIdType.MESH,
        )

    near = half + DMAX
    to_mirror = send_rows(cot.at[pl.ds(half - DMAX, near)], second_s.at[pl.ds(0, near)], 0, mirror)
    to_next = send_rows(cot.at[pl.ds(rows - DMAX, DMAX)], low_s.at[pl.ds(0, DMAX)], 1, following)
    to_beyond = send_rows(cot.at[pl.ds(0, DMAX)], second_s.at[pl.ds(near, DMAX)], 2, beyond)
    to_mirror.start()
    to_next.start()

    @pl.when(alone)
    def _():
        own_copy = pltpu.make_async_copy(
            cot.at[pl.ds(0, DMAX)], second_s.at[pl.ds(near, DMAX)], sems_c.at[0, 3]
        )
        own_copy.start()
        own_copy.wait()

    @pl.when(jnp.logical_not(alone))
    def _():
        to_beyond.start()

    low_s[DMAX:part, :] = cot[0:near, :]

    embedded = emb[...]
    wide0 = embedded.astype(F32)
    inverse0 = lax.rsqrt(jnp.mean(wide0 * wide0, axis=-1, keepdims=True) + EPSILON)
    unit0 = wide0 * inverse0
    table = (unit0 * gain[0:1, :]).astype(BF16)
    table_wide = table.astype(F32)
    tapped = jnp.concatenate([taps[0, k : k + 1, :] * table_wide for k in range(3)], axis=0)
    tapped = jnp.concatenate([tapped, jnp.zeros((4, channels), F32)], axis=0)
    up_high, up_low = parts(table_dot(tapped, up_w[0]))
    gates = jax.nn.sigmoid(dot(jnp.concatenate([table_wide] * 4, axis=0).astype(BF16), gate_w[0]))
    row_of = lax.broadcasted_iota(jnp.int32, (16, channels), 0)
    gate_high, gate_low = parts(jnp.where(row_of >= 12, gates, 0.0))
    up_table = jnp.concatenate([up_high, up_low], axis=0)
    gate_table = jnp.concatenate([gate_high, gate_low], axis=0)
    embed_table = jnp.where(
        (row_of >= 4) & (row_of < 8), jnp.concatenate([wide0] * 4, axis=0), 0.0
    ).astype(BF16)
    hot_rows = lax.broadcasted_iota(jnp.int32, (16, 128), 0)

    def hot_at(start):
        code = codes[:, pl.ds(pl.multiple_of(start, 128), 128)]
        return jnp.where(code == lax.rem(hot_rows, 4), 1.0, 0.0)

    def block0(hot):
        two = jnp.concatenate([hot, hot], axis=0).astype(BF16)
        return turned(two, up_table), turned(two, gate_table)

    first_row = lax.broadcasted_iota(jnp.int32, (128, 1), 0)

    def forward0(c, carry):
        start = pl.multiple_of(c * 128, 128)
        hot = hot_at(start)
        upward0, gate0 = block0(hot)
        hidden0 = (upward0 * gate0).astype(BF16)
        wide = turned(hot.astype(BF16), embed_table) + dot(hidden0, out_w[0])
        wide = wide.astype(BF16).astype(F32)
        inverse = lax.rsqrt(jnp.mean(wide * wide, axis=-1, keepdims=True) + EPSILON)
        unit = wide * inverse
        place = me * rows - 2 * DMAX + lax.rem(start, full) + first_row
        normed = jnp.where(place >= 0, unit * gain[1:2, :], 0.0).astype(BF16)
        at = pl.ds(start, 128)
        unit_s[at, :] = unit
        inv_s[at, :] = jnp.broadcast_to(inverse, (128, 128))
        norm_s[at, :] = normed
        return carry

    lax.fori_loop(0, 2 * full // 128, forward0, 0)

    to_mirror.wait()
    to_next.wait()

    @pl.when(jnp.logical_not(alone))
    def _():
        to_beyond.wait()

    up = lax.broadcasted_iota(jnp.int32, (part, part), 0)
    down = lax.broadcasted_iota(jnp.int32, (part, part), 1)
    flip = jnp.where(up + down == part - 1, 1.0, 0.0).astype(BF16)
    edge_row = lax.broadcasted_iota(jnp.int32, (DMAX, 1), 0)
    within = me * rows - DMAX + edge_row >= 0
    low_s[part : 2 * part, :] = dot(flip, second_s[...]).astype(BF16)
    for p in range(2):
        edge = low_s[p * part : p * part + DMAX, :].astype(F32)
        low_s[p * part : p * part + DMAX, :] = jnp.where(within, edge, 0.0).astype(BF16)

    d1 = dil[1]
    tap = [taps[1, k : k + 1, :] for k in range(3)]

    to_row = lax.broadcasted_iota(jnp.int32, (128, 256), 0)
    from_row = lax.broadcasted_iota(jnp.int32, (128, 256), 1)
    distance = from_row - to_row - DMAX

    def shifted(ref, at, offset):
        window = ref[pl.ds(pl.multiple_of(at - DMAX, 64), 256), :]
        move = jnp.where(distance == offset, 1.0, 0.0).astype(BF16)
        return dot(move, window)

    def middle(c, carry):
        p = lax.div(c, part // 128)
        r0 = lax.rem(c, part // 128) * 128
        sign = 1 - 2 * p
        begin = p * full + DMAX + r0
        mixed = tap[0] * shifted(norm_s, begin, -sign * d1)
        mixed = mixed + tap[1] * norm_s[pl.ds(pl.multiple_of(begin, 64), 128), :].astype(F32)
        mixed = (mixed + tap[2] * shifted(norm_s, begin, sign * d1)).astype(BF16)
        other = pl.multiple_of((1 - p) * full + DMAX + r0, 64)
        partner = norm_s[pl.ds(other, 128), :]
        at = pl.ds(pl.multiple_of(c * 128, 128), 128)
        upward = dot(mixed, up_w[1])
        gate = jax.nn.sigmoid(dot(partner, gate_w[1]))
        grad_hidden = dot_t(low_s[at, :], out_w[1])
        gated = grad_hidden * gate
        gu = gated.astype(BF16)
        gl = (gated * upward * (1.0 - gate)).astype(BF16)
        mixed_s[at, :] = mixed
        partner_s[at, :] = partner
        hidden_s[at, :] = (upward * gate).astype(BF16)
        gu_s[at, :] = gu
        gl_s[at, :] = gl
        gm_s[at, :] = dot_t(gu, up_w[1]).astype(BF16)
        gp_s[at, :] = dot_t(gl, gate_w[1]).astype(BF16)
        return carry

    lax.fori_loop(0, 2 * part // 128, middle, 0)

    def own(ref, cols=slice(None)):
        return jnp.concatenate(
            [ref[DMAX : DMAX + half, cols], ref[part + DMAX : part + DMAX + half, cols]], axis=0
        )

    def rows_into(mat, left, right, pick):
        whole = pick(right)
        for c in range(channels // 256):
            cols = slice(c * 256, c * 256 + 256)
            mat[cols, :] = turned(pick(left, cols), whole)

    rows_into(m_out1, low_s, hidden_s, own)
    rows_into(m_up1, gu_s, mixed_s, own)
    rows_into(m_gate1, gl_s, partner_s, own)

    order_a = list(range(steps))
    order_b = [0] + order_a[2:] + [1]
    first = Halving(n, order_a, me, (m_out1, m_up1, m_gate1), acc_a, send_a, recv_a, sems_a)
    first.start(0)

    small_out[...] = jnp.zeros_like(small_out)

    def backward(c, carry):
        p = lax.div(c, half // 128)
        r0 = lax.rem(c, half // 128) * 128
        sign = 1 - 2 * p
        mine = p * part + DMAX + r0
        mine_at = pl.ds(pl.multiple_of(mine, 64), 128)
        here = p * full + 2 * DMAX + r0
        here_at = pl.ds(pl.multiple_of(here, 64), 128)
        grad_mixed = gm_s[mine_at, :].astype(F32)
        grad_normed = tap[0] * shifted(gm_s, mine, sign * d1)
        grad_normed = grad_normed + tap[1] * grad_mixed
        grad_normed = grad_normed + tap[2] * shifted(gm_s, mine, -sign * d1)
        other = pl.multiple_of((1 - p) * part + DMAX + r0, 64)
        grad_normed = grad_normed + gp_s[pl.ds(other, 128), :].astype(F32)
        unit = unit_s[here_at, :]
        sums = [
            jnp.sum(grad_mixed * shifted(norm_s, here, -sign * d1), axis=0, keepdims=True),
            jnp.sum(grad_mixed * norm_s[here_at, :].astype(F32), axis=0, keepdims=True),
            jnp.sum(grad_mixed * shifted(norm_s, here, sign * d1), axis=0, keepdims=True),
            jnp.sum(grad_normed * unit, axis=0, keepdims=True),
            jnp.zeros((4, channels), F32),
        ]
        grad_unit = grad_normed * gain[1:2, :]
        average = jnp.mean(grad_unit * unit, axis=-1, keepdims=True)
        gradient = low_s[mine_at, :].astype(F32) + inv_s[here_at, 0:1] * (
            grad_unit - unit * average
        )
        low0, rest0 = parts(gradient)
        grad_hidden0 = dot_t(low0, out_w[0])
        hot = hot_at(here)
        upward0, gate0 = block0(hot)
        gated = grad_hidden0 * gate0
        gu0 = gated.astype(BF16)
        gl0 = (gated * upward0 * (1.0 - gate0)).astype(BF16)
        hot_up = jnp.where(hot_rows < 12, hot, 0.0).astype(BF16)
        hot_gate = jnp.where(hot_rows < 12, 0.0, hot).astype(BF16)
        hot16 = hot.astype(BF16)
        small_out[0:16, :] += dot(hot_up, gu0) + dot(hot_gate, gl0)
        small_out[16:24, :] += (dot(hot16, low0) + dot(hot16, rest0))[0:8]
        small_out[24:32, :] += jnp.concatenate(sums, axis=0)
        at = pl.ds(pl.multiple_of(c * 128, 128), 128)
        low0_s[at, :] = low0
        hidden0_s[at, :] = (upward0 * gate0).astype(BF16)
        return carry

    lax.fori_loop(0, 2 * half // 128, backward, 0)

    first.finish(0)
    first.start(1)
    rows_into(m_out0, low0_s, hidden0_s, lambda ref, cols=slice(None): ref[:, cols])
    second = Halving(n, order_b, me, (m_out0,), acc_b, send_b, recv_b, sems_b)

    def small_copy(j):
        partner = second.plan(j)[2]
        return pltpu.make_async_remote_copy(
            src_ref=ssend.at[j], dst_ref=srecv.at[j],
            send_sem=sems_s.at[0, j], recv_sem=sems_s.at[1, j],
            device_id={"seq": partner}, device_id_type=pl.DeviceIdType.MESH,
        )

    for j in range(steps):
        ssend[j] = small_out[...]
        small_copy(j).start()
        second.start(j)
        if j + 1 < steps:
            if j > 0:
                first.start(j + 1)
            first.finish(j + 1) if j == 0 else None
        small_copy(j).wait()
        small_out[...] = small_out[...] + srecv[j]
        second.finish(j)
        if 0 < j and j + 1 < steps:
            first.finish(j + 1)
    out_a[...] = acc_a[0]
    out_b[...] = acc_b[0]

    sums = small_out[0:16, :]
    width = channels // n
    pick = jnp.where(
        lax.broadcasted_iota(jnp.int32, (width, channels), 1)
        == me * width + lax.broadcasted_iota(jnp.int32, (width, channels), 0),
        1.0,
        0.0,
    )

    def exact(a, b, dims):
        return lax.dot_general(
            a, b, (dims, ((), ())), precision=lax.Precision.HIGHEST, preferred_element_type=F32
        )

    mine = exact(pick, sums, ((1,), (1,)))
    gate_rows = jnp.where(row_of >= 12, jnp.concatenate([table_wide] * 4, axis=0), 0.0)
    out_c[0:width, :] = exact(mine, tapped, ((1,), (0,)))
    out_c[width : 2 * width, :] = exact(mine, gate_rows, ((1,), (0,)))
    spread = table_dot(sums, up_w[0], True)
    grad_normed0 = table_dot(sums, gate_w[0], True)[12:16]
    for k in range(3):
        own_rows = spread[4 * k : 4 * k + 4]
        grad_normed0 = grad_normed0 + taps[0, k : k + 1, :] * own_rows
        out_taps[0, k : k + 1, :] = jnp.sum(own_rows * table_wide, axis=0, keepdims=True)
    out_taps[1] = small_out[24:27, :]
    out_gain[0:1, :] = jnp.sum(grad_normed0 * unit0, axis=0, keepdims=True)
    out_gain[1:2, :] = small_out[27:28, :]
    grad_unit0 = grad_normed0 * gain[0:1, :]
    out_embed[...] = small_out[20:24, :] + inverse0 * (
        grad_unit0 - unit0 * jnp.mean(grad_unit0 * unit0, axis=-1, keepdims=True)
    )


def fused(dilations, codes, embedding, norm_gain, conv_taps, w_up, w_gate, w_out, cotangent):
    n = lax.axis_size("seq")
    steps = n.bit_length() - 1
    rows, channels = cotangent.shape
    half = rows // 2
    full, part = 2 * (half + 4 * DMAX), 2 * (half + 2 * DMAX)
    width = channels // n
    vmem = pl.BlockSpec(memory_space=pltpu.VMEM)

    def wide(count, kind=F32, cols=channels):
        return pltpu.VMEM((count, cols), kind)

    def buffers(mats):
        return [
            pltpu.VMEM((n // 2, mats * width, channels), F32),
            pltpu.VMEM((n - 1, mats * width, channels), BF16 if mats * width % 16 == 0 else F32),
            pltpu.VMEM((n - 1, mats * width, channels), BF16 if mats * width % 16 == 0 else F32),
        ]

    sems = pltpu.SemaphoreType.DMA
    return pl.pallas_call(
        functools.partial(kernel, n, steps),
        out_shape=(
            jax.ShapeDtypeStruct((3 * width, channels), F32),
            jax.ShapeDtypeStruct((width, channels), F32),
            jax.ShapeDtypeStruct((2 * width, channels), F32),
            jax.ShapeDtypeStruct(conv_taps.shape, F32),
            jax.ShapeDtypeStruct(norm_gain.shape, F32),
            jax.ShapeDtypeStruct(embedding.shape, F32),
        ),
        in_specs=[pl.BlockSpec(memory_space=pltpu.SMEM)] + [vmem] * 8,
        out_specs=(vmem,) * 6,
        scratch_shapes=[
            wide(32), wide(part, BF16), wide(part // 2, BF16),
            wide(full), wide(full, F32, 128), wide(full, BF16),
            *[wide(part, BF16) for _ in range(5)],
            wide(part, BF16), wide(part, BF16),
            wide(2 * half, BF16), wide(2 * half, BF16),
            *[wide(channels) for _ in range(4)],
            *buffers(3), *buffers(1),
            pltpu.VMEM((steps, 32, channels), F32), pltpu.VMEM((steps, 32, channels), F32),
            sems((2, steps)), sems((2, steps)), sems((2, steps)), sems((2, 4)),
        ],
        compiler_params=pltpu.CompilerParams(
            collective_id=0, has_side_effects=True, vmem_limit_bytes=56 * 1024 * 1024
        ),
    )(dilations, codes, embedding, norm_gain, conv_taps, w_up, w_gate, w_out, cotangent)


def per_device(tokens, dilations, embedding, norm_gain, conv_taps, w_up, w_gate, w_out, cotangent):
    n = lax.axis_size("seq")
    me = lax.axis_index("seq")
    rows = tokens.shape[0]
    half = rows // 2
    channels = embedding.shape[1]
    to_mirror = [(i, n - 1 - i) for i in range(n)]
    to_next = [(i, (i + 1) % n) for i in range(n)]
    to_beyond = [(i, (n - i) % n) for i in range(n)]

    tok_prev = lax.ppermute(tokens, "seq", to_next)
    tok_mirror = lax.ppermute(tokens, "seq", to_mirror)
    tok_beyond = lax.ppermute(tokens, "seq", to_beyond)
    edge = 3 * DMAX
    tok = jnp.stack(
        [
            jnp.concatenate([tok_prev[rows - edge :], tokens[: half + edge]]),
            jnp.flip(jnp.concatenate([tok_mirror[half - edge :], tok_beyond[:edge]])),
        ]
    )
    position = me * rows - edge + jnp.arange(half + 2 * edge, dtype=jnp.int32)
    inside = position >= 0
    tok = jnp.where(inside[None], tok, -1)
    d0 = dilations[0]
    count1 = half + 4 * DMAX
    codes = []
    for k in range(3):
        shift = (k - 1) * d0
        codes.append(
            jnp.concatenate(
                [
                    lax.dynamic_slice_in_dim(tok[0], DMAX + shift, count1, 0),
                    lax.dynamic_slice_in_dim(tok[1], DMAX - shift, count1, 0),
                ]
            )
        )
    codes.append(tok[::-1, DMAX : DMAX + count1].reshape(-1))
    codes = jnp.repeat(jnp.stack(codes), 4, axis=0)
    mats, mat_b, mat_c, grad_taps, grad_gain, grad_embed = fused(
        dilations, codes, embedding, norm_gain, conv_taps, w_up, w_gate, w_out, cotangent
    )
    width = channels // n
    out1, up1, gate1 = mats.reshape(3, width, channels)
    up0, gate0 = mat_c.reshape(2, width, channels)
    grad_up = jnp.stack([up0, up1]).transpose(0, 2, 1)
    grad_gate = jnp.stack([gate0, gate1]).transpose(0, 2, 1)
    grad_out = jnp.stack([mat_b, out1]).transpose(0, 2, 1)
    return (grad_up, grad_gate, grad_out, grad_taps, grad_gain, grad_embed)


def solution(mesh):
    in_specs = (P(("groups", "seq")), P(), P(), P(), P(), P(), P(), P(), P(("groups", "seq"), None))
    out_specs = (
        P("groups", None, "seq"),
        P("groups", None, "seq"),
        P("groups", None, "seq"),
        P("groups", None, None),
        P("groups", None),
        P("groups", None),
    )
    return jax.shard_map(
        per_device, mesh=mesh, in_specs=in_specs, out_specs=out_specs, check_vma=False
    )
```

```python
import functools

import jax
import jax.numpy as jnp
from jax import lax
from jax.experimental import pallas as pl
from jax.experimental.pallas import tpu as pltpu
from jax.sharding import PartitionSpec as P

DMAX = 64
EPSILON = 1e-06
F32 = jnp.float32
BF16 = jnp.bfloat16


def turned(a, b):
    return lax.dot_general(a, b, (((0,), (0,)), ((), ())), preferred_element_type=F32)


def dot(a, b):
    return jnp.dot(a, b, preferred_element_type=F32)


def dot_t(a, b):
    return lax.dot_general(a, b, (((1,), (1,)), ((), ())), preferred_element_type=F32)


def parts(a):
    high = a.astype(BF16)
    return high, (a - high.astype(F32)).astype(BF16)


def table_dot(table, w, transposed=False):
    high, low = parts(table)
    both = jnp.concatenate([high, low], axis=0)
    product = dot_t(both, w) if transposed else dot(both, w)
    return product[: table.shape[0]] + product[table.shape[0] :]


class Halving:
    def __init__(self, n, order, me, mats, acc, send, recv, sems):
        self.n, self.order, self.me, self.mats = n, order, me, mats
        self.acc, self.send, self.recv, self.sems = acc, send, recv, sems
        self.left = sorted(order)
        self.base = 0

    def plan(self, j):
        bit_at = self.order[j]
        at = self.left.index(bit_at)
        bit = lax.rem(lax.div(self.me, 1 << bit_at), 2)
        return at, bit, self.me + (1 - 2 * bit) * (1 << bit_at), self.n >> (j + 1)

    def block(self, j, q, at, bit):
        low = 1 << at
        index = lax.div(q, low) * (2 * low) + bit * low + lax.rem(q, low)
        if j > 0:
            return self.acc[index]
        width = self.mats[0].shape[0] // self.n
        rows = pl.ds(pl.multiple_of(index * width, width), width)
        return jnp.concatenate([m[rows, :] for m in self.mats], axis=0)

    def copy(self, j):
        at, bit, partner, count = self.plan(j)
        where = pl.ds(self.base, count)
        return pltpu.make_async_remote_copy(
            src_ref=self.send.at[where],
            dst_ref=self.recv.at[where],
            send_sem=self.sems.at[0, j],
            recv_sem=self.sems.at[1, j],
            device_id={"seq": partner},
            device_id_type=pl.DeviceIdType.MESH,
        )

    def start(self, j):
        at, bit, partner, count = self.plan(j)
        base = self.base

        def pack(q, carry):
            self.send[base + q] = self.block(j, q, at, 1 - bit).astype(self.send.dtype)
            return carry

        lax.fori_loop(0, count, pack, 0)
        self.copy(j).start()

    def finish(self, j):
        at, bit, partner, count = self.plan(j)
        base = self.base
        self.copy(j).wait()

        def fold(q, carry):
            self.acc[q] = self.block(j, q, at, bit) + self.recv[base + q].astype(F32)
            return carry

        lax.fori_loop(0, count, fold, 0)
        self.base += count
        self.left.remove(self.order[j])


def kernel(
    n, steps, dil, codes, emb, gain, taps, up_w, gate_w, out_w, cot,
    out_a, out_b, out_c, out_taps, out_gain, out_embed,
    small_out,
    low_s, second_s, unit_s, inv_s, norm_s, mixed_s, partner_s, hidden_s, gu_s, gl_s, gm_s, gp_s,
    low0_s, hidden0_s, m_out1, m_up1, m_gate1, m_out0,
    acc_a, send_a, recv_a, acc_b, send_b, recv_b, ssend, srecv,
    sems_a, sems_b, sems_s, sems_c,
):
    me = lax.axis_index("seq")
    rows, channels = cot.shape
    half = rows // 2
    full, part = half + 4 * DMAX, half + 2 * DMAX
    mirror = n - 1 - me
    following = lax.rem(me + 1, n)
    previous = lax.rem(me + n - 1, n)
    beyond = lax.rem(n - me, n)
    alone = beyond == me

    barrier = pltpu.get_barrier_semaphore()

    def greet(device):
        pl.semaphore_signal(
            barrier, inc=1, device_id={"seq": device}, device_id_type=pl.DeviceIdType.MESH
        )

    for j in range(steps):
        greet(me + (1 - 2 * lax.rem(lax.div(me, 1 << j), 2)) * (1 << j))
    greet(mirror)
    greet(following)
    greet(previous)

    @pl.when(jnp.logical_not(alone))
    def _():
        greet(beyond)

    pl.semaphore_wait(barrier, steps + 4 - jnp.where(alone, 1, 0))

    def send_rows(src, dst, at, device):
        return pltpu.make_async_remote_copy(
            src_ref=src, dst_ref=dst, send_sem=sems_c.at[0, at], recv_sem=sems_c.at[1, at],
            device_id={"seq": device}, device_id_type=pl.DeviceIdType.MESH,
        )

    near = half + DMAX
    to_mirror = send_rows(cot.at[pl.ds(half - DMAX, near)], second_s.at[pl.ds(0, near)], 0, mirror)
    to_next = send_rows(cot.at[pl.ds(rows - DMAX, DMAX)], low_s.at[pl.ds(0, DMAX)], 1, following)
    to_beyond = send_rows(cot.at[pl.ds(0, DMAX)], second_s.at[pl.ds(near, DMAX)], 2, beyond)
    to_mirror.start()
    to_next.start()

    @pl.when(alone)
    def _():
        own_copy = pltpu.make_async_copy(
            cot.at[pl.ds(0, DMAX)], second_s.at[pl.ds(near, DMAX)], sems_c.at[0, 3]
        )
        own_copy.start()
        own_copy.wait()

    @pl.when(jnp.logical_not(alone))
    def _():
        to_beyond.start()

    low_s[DMAX:part, :] = cot[0:near, :]

    embedded = emb[...]
    wide0 = embedded.astype(F32)
    inverse0 = lax.rsqrt(jnp.mean(wide0 * wide0, axis=-1, keepdims=True) + EPSILON)
    unit0 = wide0 * inverse0
    table = (unit0 * gain[0:1, :]).astype(BF16)
    table_wide = table.astype(F32)
    tapped = jnp.concatenate([taps[0, k : k + 1, :] * table_wide for k in range(3)], axis=0)
    tapped = jnp.concatenate([tapped, jnp.zeros((4, channels), F32)], axis=0)
    up_high, up_low = parts(table_dot(tapped, up_w[0]))
    gates = jax.nn.sigmoid(dot(jnp.concatenate([table_wide] * 4, axis=0).astype(BF16), gate_w[0]))
    row_of = lax.broadcasted_iota(jnp.int32, (16, channels), 0)
    gate_high, gate_low = parts(jnp.where(row_of >= 12, gates, 0.0))
    up_table = jnp.concatenate([up_high, up_low], axis=0)
    gate_table = jnp.concatenate([gate_high, gate_low], axis=0)
    embed_table = jnp.where(
        (row_of >= 4) & (row_of < 8), jnp.concatenate([wide0] * 4, axis=0), 0.0
    ).astype(BF16)
    hot_rows = lax.broadcasted_iota(jnp.int32, (16, 128), 0)

    def hot_at(start):
        code = codes[:, pl.ds(pl.multiple_of(start, 128), 128)]
        return jnp.where(code == lax.rem(hot_rows, 4), 1.0, 0.0)

    def block0(hot):
        two = jnp.concatenate([hot, hot], axis=0).astype(BF16)
        return turned(two, up_table), turned(two, gate_table)

    first_row = lax.broadcasted_iota(jnp.int32, (128, 1), 0)

    def forward0(c, carry):
        start = pl.multiple_of(c * 128, 128)
        hot = hot_at(start)
        upward0, gate0 = block0(hot)
        hidden0 = (upward0 * gate0).astype(BF16)
        wide = turned(hot.astype(BF16), embed_table) + dot(hidden0, out_w[0])
        wide = wide.astype(BF16).astype(F32)
        inverse = lax.rsqrt(jnp.mean(wide * wide, axis=-1, keepdims=True) + EPSILON)
        unit = wide * inverse
        place = me * rows - 2 * DMAX + lax.rem(start, full) + first_row
        normed = jnp.where(place >= 0, unit * gain[1:2, :], 0.0).astype(BF16)
        at = pl.ds(start, 128)
        unit_s[at, :] = unit
        inv_s[at, :] = jnp.broadcast_to(inverse, (128, 128))
        norm_s[at, :] = normed
        return carry

    lax.fori_loop(0, 2 * full // 128, forward0, 0)

    to_mirror.wait()
    to_next.wait()

    @pl.when(jnp.logical_not(alone))
    def _():
        to_beyond.wait()

    up = lax.broadcasted_iota(jnp.int32, (part, part), 0)
    down = lax.broadcasted_iota(jnp.int32, (part, part), 1)
    flip = jnp.where(up + down == part - 1, 1.0, 0.0).astype(BF16)
    edge_row = lax.broadcasted_iota(jnp.int32, (DMAX, 1), 0)
    within = me * rows - DMAX + edge_row >= 0
    low_s[part : 2 * part, :] = dot(flip, second_s[...]).astype(BF16)
    for p in range(2):
        edge = low_s[p * part : p * part + DMAX, :].astype(F32)
        low_s[p * part : p * part + DMAX, :] = jnp.where(within, edge, 0.0).astype(BF16)

    d1 = dil[1]
    tap = [taps[1, k : k + 1, :] for k in range(3)]

    to_row = lax.broadcasted_iota(jnp.int32, (128, 256), 0)
    from_row = lax.broadcasted_iota(jnp.int32, (128, 256), 1)
    distance = from_row - to_row - DMAX

    def shifted(ref, at, offset):
        window = ref[pl.ds(pl.multiple_of(at - DMAX, 64), 256), :]
        move = jnp.where(distance == offset, 1.0, 0.0).astype(BF16)
        return dot(move, window)

    def middle(c, carry):
        p = lax.div(c, part // 128)
        r0 = lax.rem(c, part // 128) * 128
        sign = 1 - 2 * p
        begin = p * full + DMAX + r0
        mixed = tap[0] * shifted(norm_s, begin, -sign * d1)
        mixed = mixed + tap[1] * norm_s[pl.ds(pl.multiple_of(begin, 64), 128), :].astype(F32)
        mixed = (mixed + tap[2] * shifted(norm_s, begin, sign * d1)).astype(BF16)
        other = pl.multiple_of((1 - p) * full + DMAX + r0, 64)
        partner = norm_s[pl.ds(other, 128), :]
        at = pl.ds(pl.multiple_of(c * 128, 128), 128)
        upward = dot(mixed, up_w[1])
        gate = jax.nn.sigmoid(dot(partner, gate_w[1]))
        grad_hidden = dot_t(low_s[at, :], out_w[1])
        gated = grad_hidden * gate
        gu = gated.astype(BF16)
        gl = (gated * upward * (1.0 - gate)).astype(BF16)
        mixed_s[at, :] = mixed
        partner_s[at, :] = partner
        hidden_s[at, :] = (upward * gate).astype(BF16)
        gu_s[at, :] = gu
        gl_s[at, :] = gl
        gm_s[at, :] = dot_t(gu, up_w[1]).astype(BF16)
        gp_s[at, :] = dot_t(gl, gate_w[1]).astype(BF16)
        return carry

    lax.fori_loop(0, 2 * part // 128, middle, 0)

    def own(ref, cols=slice(None)):
        return jnp.concatenate(
            [ref[DMAX : DMAX + half, cols], ref[part + DMAX : part + DMAX + half, cols]], axis=0
        )

    def rows_into(mat, left, right, pick):
        whole = pick(right)
        for c in range(channels // 256):
            cols = slice(c * 256, c * 256 + 256)
            mat[cols, :] = turned(pick(left, cols), whole)

    rows_into(m_out1, low_s, hidden_s, own)
    rows_into(m_up1, gu_s, mixed_s, own)
    rows_into(m_gate1, gl_s, partner_s, own)

    order_a = list(range(steps))
    order_b = [0] + order_a[2:] + [1]
    first = Halving(n, order_a, me, (m_out1, m_up1, m_gate1), acc_a, send_a, recv_a, sems_a)
    first.start(0)

    small_out[...] = jnp.zeros_like(small_out)

    def backward(c, carry):
        p = lax.div(c, half // 128)
        r0 = lax.rem(c, half // 128) * 128
        sign = 1 - 2 * p
        mine = p * part + DMAX + r0
        mine_at = pl.ds(pl.multiple_of(mine, 64), 128)
        here = p * full + 2 * DMAX + r0
        here_at = pl.ds(pl.multiple_of(here, 64), 128)
        grad_mixed = gm_s[mine_at, :].astype(F32)
        grad_normed = tap[0] * shifted(gm_s, mine, sign * d1)
        grad_normed = grad_normed + tap[1] * grad_mixed
        grad_normed = grad_normed + tap[2] * shifted(gm_s, mine, -sign * d1)
        other = pl.multiple_of((1 - p) * part + DMAX + r0, 64)
        grad_normed = grad_normed + gp_s[pl.ds(other, 128), :].astype(F32)
        unit = unit_s[here_at, :]
        sums = [
            jnp.sum(grad_mixed * shifted(norm_s, here, -sign * d1), axis=0, keepdims=True),
            jnp.sum(grad_mixed * norm_s[here_at, :].astype(F32), axis=0, keepdims=True),
            jnp.sum(grad_mixed * shifted(norm_s, here, sign * d1), axis=0, keepdims=True),
            jnp.sum(grad_normed * unit, axis=0, keepdims=True),
            jnp.zeros((4, channels), F32),
        ]
        grad_unit = grad_normed * gain[1:2, :]
        average = jnp.mean(grad_unit * unit, axis=-1, keepdims=True)
        gradient = low_s[mine_at, :].astype(F32) + inv_s[here_at, 0:1] * (
            grad_unit - unit * average
        )
        low0, rest0 = parts(gradient)
        grad_hidden0 = dot_t(low0, out_w[0])
        hot = hot_at(here)
        upward0, gate0 = block0(hot)
        gated = grad_hidden0 * gate0
        gu0 = gated.astype(BF16)
        gl0 = (gated * upward0 * (1.0 - gate0)).astype(BF16)
        hot_up = jnp.where(hot_rows < 12, hot, 0.0).astype(BF16)
        hot_gate = jnp.where(hot_rows < 12, 0.0, hot).astype(BF16)
        hot16 = hot.astype(BF16)
        small_out[0:16, :] += dot(hot_up, gu0) + dot(hot_gate, gl0)
        small_out[16:24, :] += (dot(hot16, low0) + dot(hot16, rest0))[0:8]
        small_out[24:32, :] += jnp.concatenate(sums, axis=0)
        at = pl.ds(pl.multiple_of(c * 128, 128), 128)
        low0_s[at, :] = low0
        hidden0_s[at, :] = (upward0 * gate0).astype(BF16)
        return carry

    lax.fori_loop(0, 1, backward, 0)
    first.finish(0)
    first.start(1)
    lax.fori_loop(1, 2 * half // 128, backward, 0)
    rows_into(m_out0, low0_s, hidden0_s, lambda ref, cols=slice(None): ref[:, cols])
    second = Halving(n, order_b, me, (m_out0,), acc_b, send_b, recv_b, sems_b)

    def small_copy(j):
        partner = second.plan(j)[2]
        return pltpu.make_async_remote_copy(
            src_ref=ssend.at[j], dst_ref=srecv.at[j],
            send_sem=sems_s.at[0, j], recv_sem=sems_s.at[1, j],
            device_id={"seq": partner}, device_id_type=pl.DeviceIdType.MESH,
        )

    for j in range(steps):
        ssend[j] = small_out[...]
        small_copy(j).start()
        second.start(j)
        if j > 0:
            first.finish(j)
            if j + 1 < steps:
                first.start(j + 1)
        small_copy(j).wait()
        small_out[...] = small_out[...] + srecv[j]
        second.finish(j)
    out_a[...] = acc_a[0]
    out_b[...] = acc_b[0]

    sums = small_out[0:16, :]
    width = channels // n
    pick = jnp.where(
        lax.broadcasted_iota(jnp.int32, (width, channels), 1)
        == me * width + lax.broadcasted_iota(jnp.int32, (width, channels), 0),
        1.0,
        0.0,
    )

    def exact(a, b, dims):
        return lax.dot_general(
            a, b, (dims, ((), ())), precision=lax.Precision.HIGHEST, preferred_element_type=F32
        )

    mine = exact(pick, sums, ((1,), (1,)))
    gate_rows = jnp.where(row_of >= 12, jnp.concatenate([table_wide] * 4, axis=0), 0.0)
    out_c[0:width, :] = exact(mine, tapped, ((1,), (0,)))
    out_c[width : 2 * width, :] = exact(mine, gate_rows, ((1,), (0,)))
    spread = table_dot(sums, up_w[0], True)
    grad_normed0 = table_dot(sums, gate_w[0], True)[12:16]
    for k in range(3):
        own_rows = spread[4 * k : 4 * k + 4]
        grad_normed0 = grad_normed0 + taps[0, k : k + 1, :] * own_rows
        out_taps[0, k : k + 1, :] = jnp.sum(own_rows * table_wide, axis=0, keepdims=True)
    out_taps[1] = small_out[24:27, :]
    out_gain[0:1, :] = jnp.sum(grad_normed0 * unit0, axis=0, keepdims=True)
    out_gain[1:2, :] = small_out[27:28, :]
    grad_unit0 = grad_normed0 * gain[0:1, :]
    out_embed[...] = small_out[20:24, :] + inverse0 * (
        grad_unit0 - unit0 * jnp.mean(grad_unit0 * unit0, axis=-1, keepdims=True)
    )


def fused(dilations, codes, embedding, norm_gain, conv_taps, w_up, w_gate, w_out, cotangent):
    n = lax.axis_size("seq")
    steps = n.bit_length() - 1
    rows, channels = cotangent.shape
    half = rows // 2
    full, part = 2 * (half + 4 * DMAX), 2 * (half + 2 * DMAX)
    width = channels // n
    vmem = pl.BlockSpec(memory_space=pltpu.VMEM)

    def wide(count, kind=F32, cols=channels):
        return pltpu.VMEM((count, cols), kind)

    def buffers(mats):
        return [
            pltpu.VMEM((n // 2, mats * width, channels), F32),
            pltpu.VMEM((n - 1, mats * width, channels), BF16 if mats * width % 16 == 0 else F32),
            pltpu.VMEM((n - 1, mats * width, channels), BF16 if mats * width % 16 == 0 else F32),
        ]

    sems = pltpu.SemaphoreType.DMA
    return pl.pallas_call(
        functools.partial(kernel, n, steps),
        out_shape=(
            jax.ShapeDtypeStruct((3 * width, channels), F32),
            jax.ShapeDtypeStruct((width, channels), F32),
            jax.ShapeDtypeStruct((2 * width, channels), F32),
            jax.ShapeDtypeStruct(conv_taps.shape, F32),
            jax.ShapeDtypeStruct(norm_gain.shape, F32),
            jax.ShapeDtypeStruct(embedding.shape, F32),
        ),
        in_specs=[pl.BlockSpec(memory_space=pltpu.SMEM)] + [vmem] * 8,
        out_specs=(vmem,) * 6,
        scratch_shapes=[
            wide(32), wide(part, BF16), wide(part // 2, BF16),
            wide(full), wide(full, F32, 128), wide(full, BF16),
            *[wide(part, BF16) for _ in range(5)],
            wide(part, BF16), wide(part, BF16),
            wide(2 * half, BF16), wide(2 * half, BF16),
            *[wide(channels) for _ in range(4)],
            *buffers(3), *buffers(1),
            pltpu.VMEM((steps, 32, channels), F32), pltpu.VMEM((steps, 32, channels), F32),
            sems((2, steps)), sems((2, steps)), sems((2, steps)), sems((2, 4)),
        ],
        compiler_params=pltpu.CompilerParams(
            collective_id=0, has_side_effects=True, vmem_limit_bytes=56 * 1024 * 1024
        ),
    )(dilations, codes, embedding, norm_gain, conv_taps, w_up, w_gate, w_out, cotangent)


def per_device(tokens, dilations, embedding, norm_gain, conv_taps, w_up, w_gate, w_out, cotangent):
    n = lax.axis_size("seq")
    me = lax.axis_index("seq")
    rows = tokens.shape[0]
    half = rows // 2
    channels = embedding.shape[1]
    to_mirror = [(i, n - 1 - i) for i in range(n)]
    to_next = [(i, (i + 1) % n) for i in range(n)]
    to_beyond = [(i, (n - i) % n) for i in range(n)]

    tok_prev = lax.ppermute(tokens, "seq", to_next)
    tok_mirror = lax.ppermute(tokens, "seq", to_mirror)
    tok_beyond = lax.ppermute(tokens, "seq", to_beyond)
    edge = 3 * DMAX
    tok = jnp.stack(
        [
            jnp.concatenate([tok_prev[rows - edge :], tokens[: half + edge]]),
            jnp.flip(jnp.concatenate([tok_mirror[half - edge :], tok_beyond[:edge]])),
        ]
    )
    position = me * rows - edge + jnp.arange(half + 2 * edge, dtype=jnp.int32)
    inside = position >= 0
    tok = jnp.where(inside[None], tok, -1)
    d0 = dilations[0]
    count1 = half + 4 * DMAX
    codes = []
    for k in range(3):
        shift = (k - 1) * d0
        codes.append(
            jnp.concatenate(
                [
                    lax.dynamic_slice_in_dim(tok[0], DMAX + shift, count1, 0),
                    lax.dynamic_slice_in_dim(tok[1], DMAX - shift, count1, 0),
                ]
            )
        )
    codes.append(tok[::-1, DMAX : DMAX + count1].reshape(-1))
    codes = jnp.repeat(jnp.stack(codes), 4, axis=0)
    mats, mat_b, mat_c, grad_taps, grad_gain, grad_embed = fused(
        dilations, codes, embedding, norm_gain, conv_taps, w_up, w_gate, w_out, cotangent
    )
    width = channels // n
    out1, up1, gate1 = mats.reshape(3, width, channels)
    up0, gate0 = mat_c.reshape(2, width, channels)
    grad_up = jnp.stack([up0, up1]).transpose(0, 2, 1)
    grad_gate = jnp.stack([gate0, gate1]).transpose(0, 2, 1)
    grad_out = jnp.stack([mat_b, out1]).transpose(0, 2, 1)
    return (grad_up, grad_gate, grad_out, grad_taps, grad_gain, grad_embed)


def solution(mesh):
    in_specs = (P(("groups", "seq")), P(), P(), P(), P(), P(), P(), P(), P(("groups", "seq"), None))
    out_specs = (
        P("groups", None, "seq"),
        P("groups", None, "seq"),
        P("groups", None, "seq"),
        P("groups", None, None),
        P("groups", None),
        P("groups", None),
    )
    return jax.shard_map(
        per_device, mesh=mesh, in_specs=in_specs, out_specs=out_specs, check_vma=False
    )
```
